128 devices in a mesh: shard: 128 (over x, z, y, core).
Axes of the slice: x: 4, y: 4, z: 4, core: 2. Of those that a mesh axis runs over, the one named last changes fastest.
Arguments:
- grads: float32 [384, 65536], P(None, 'shard'), may hold values from -1200 to 1200
- owner: int32 [384, 1], replicated, may hold values from 0 to 127; in each aligned block of 384 rows (0 to 383, 384 to 767, ...) at most 8 rows name the same one
- left_stat: float32 [1024, 256, 256], P('shard'), may hold values from -60 to 640, as said below
- right_stat: float32 [1024, 256, 256], P('shard'), may hold values from -60 to 640, as said below
- left_root: bfloat16 [1024, 256, 256], P('shard'), may hold values from -1 to 2.5, as said below
- right_root: bfloat16 [1024, 256, 256], P('shard'), may hold values from -1 to 2.5, as said below
- moment: float32 [1024, 256, 256], P('shard'), may hold values from 0.1 to 10
Outputs:
- update: float32 [384, 65536], P(None, 'shard')
- left_new: float32 [1024, 256, 256], P('shard')
- right_new: float32 [1024, 256, 256], P('shard')
- moment_new: float32 [1024, 256, 256], P('shard')
The draws below stay inside these ranges and needn't reach their ends.
Inputs may be any that keep to these rules, and one draw needn't show every extreme that they name: Every owner is named by at least one tile and by at most 8 tiles; some owner by exactly 8. `left_stat`: each matrix is symmetric. `right_stat`: each matrix is symmetric. `left_root`: each matrix is symmetric. `right_root`: each matrix is symmetric.
All inputs are finite; a program needn't handle non-finite values.
Results may differ from the reference program's by a relative error of at most 0.0041.
Values sent between devices are 32-bit elements; how exact they have to be, the bound alone decides.
No kernel may reach another device: no remote copies, remote signals or barrier semaphores. Data moves between devices by JAX's collectives and lax.ppermute only.
A program may use at most 64 MiB of HBM per device.

```python
import math
import jax
import jax.numpy as jnp
import numpy as np
from jax import lax

B = 256
SLOT_DEV = 8
TILES = 384
SLOTS = 1024
N_SHARD = 128


def symmetric_draw(key, lowest, highest, spread):
    streams = jax.random.split(key, 2)
    diagonal = jnp.exp(jax.random.uniform(streams[0], (SLOTS, B), jnp.float32, math.log(lowest), math.log(highest)))
    gaussian = jnp.clip(jax.random.normal(streams[1], (SLOTS, B, B), jnp.float32), -3.0, 3.0)
    offdiag = spread * (gaussian + jnp.swapaxes(gaussian, 1, 2))
    eye_mask = jnp.eye(B, dtype=jnp.float32)
    return offdiag * (1.0 - eye_mask) + diagonal[:, :, None] * eye_mask


def draw_grads(key, part):
    key = jax.random.fold_in(key, 11)
    streams = jax.random.split(key, 3)
    entries = jnp.clip(jax.random.normal(streams[0], (TILES, B, B), jnp.float32), -4.0, 4.0)
    row_scale = jnp.exp(jax.random.uniform(streams[1], (TILES, B, 1), jnp.float32, 0.0, math.log(10.0)))
    col_scale = jnp.exp(jax.random.uniform(streams[2], (TILES, 1, B), jnp.float32, 0.0, math.log(10.0)))
    rising = 1.0 + 2.0 * jnp.arange(B * B, dtype=jnp.float32).reshape(1, B, B) / (B * B)
    return (entries * row_scale * col_scale * rising).reshape(TILES, B * B)


def draw_left_stat(key, part):
    key = jax.random.fold_in(key, 21)
    return symmetric_draw(key, 64.0, 580.0, 10.0)


def draw_right_stat(key, part):
    key = jax.random.fold_in(key, 31)
    return symmetric_draw(key, 64.0, 580.0, 10.0)


def draw_left_root(key, part):
    key = jax.random.fold_in(key, 41)
    return symmetric_draw(key, 0.5, 2.0, 0.5 / math.sqrt(2.0 * B)).astype(jnp.bfloat16)


def draw_right_root(key, part):
    key = jax.random.fold_in(key, 51)
    return symmetric_draw(key, 0.5, 2.0, 0.5 / math.sqrt(2.0 * B)).astype(jnp.bfloat16)


def block_levels(key, dims, shards, least, largest):
    factor_of = 1.0
    for axis_at, blocks in shards:
        draws = jax.random.uniform(jax.random.fold_in(jax.random.fold_in(key, 6), axis_at), (blocks,), jnp.float32, least / len(shards), largest / len(shards))
        factor_of = factor_of * jnp.repeat(jnp.exp(draws), dims[axis_at] // blocks).reshape((-1,) + (1,) * (len(dims) - 1 - axis_at))
    return factor_of


def assign_block(own_key, own, number, rows, amount, top, most, lean):
    sequence = jax.random.permutation(own_key, amount)
    packed, common = shares(amount, rows * top, most, lean, True), shares(amount, rows * top, most, lean, False)
    places = jnp.arange(amount)

    def named(lengths, turn):
        used = int((lengths > 0).sum())
        fixed = max(1, used // 4)
        passed = fixed + (places - fixed + turn * (used - fixed)) % max(1, amount - fixed)
        return jnp.zeros((amount,), jnp.int32).at[sequence[jnp.where(places < fixed, places, passed)]].set(jnp.asarray(lengths, jnp.int32))

    lengths = jnp.where(number % 4 == 0, named(packed, number // 4), named(common, number - number // 4 - 1))
    mixed = jax.random.permutation(jax.random.fold_in(own, 3), amount)
    donor, taker = mixed[0:amount // 2 * 2:2], mixed[1:amount // 2 * 2:2]
    margin = jnp.minimum(lengths[donor] - 1, most - lengths[taker]) // 2
    margin = jnp.where((donor == sequence[0]) | (taker == sequence[0]) | (lengths[taker] == 0), 0, jnp.maximum(margin, 0))
    passed = jax.random.randint(jax.random.fold_in(own, 4), (amount // 2,), 0, 1 << 20) % (margin + 1)
    lengths = lengths.at[donor].add(-passed).at[taker].add(passed)
    members = jnp.searchsorted(jnp.cumsum(lengths), jnp.arange(rows * top), side="right").astype(jnp.int32)
    grid = members.reshape(top, rows).T
    grid = grid[jax.random.permutation(jax.random.fold_in(own, 1), rows)]
    turn = jax.random.randint(jax.random.fold_in(own, 2), (rows, 1), 0, top)
    return jnp.take_along_axis(grid, (jnp.arange(top)[None, :] + turn) % top, axis=1)


def shares(number_of, total, bound, slope, full):
    weights = [(1 << 20) // math.isqrt(standing ** slope) + 1 for standing in range(1, number_of + 1)]
    largest = bound if full else min(bound, max(-(-total // number_of), total * weights[0] // sum(weights)))
    least = 1 if total - largest >= number_of - 1 else 0
    given, surplus = [largest] + [least] * (number_of - 1), total - largest - least * (number_of - 1)
    while surplus > 0:
        free = [i for i in range(1, number_of) if given[i] < largest] or [i for i in range(1, number_of) if given[i] < bound]
        pool, budget = sum([weights[i] for i in free]), surplus
        for i in free:
            more = min(bound - given[i], max(1, budget * weights[i] // pool), surplus)
            given[i] = given[i] + more
            surplus = surplus - more
    return np.array(given)


def setup_inputs(seed: int = 0) -> dict:
    arg_keys = jax.random.split(jax.random.key(seed), 8)
    grads = draw_grads(jax.random.fold_in(arg_keys[7], 71), 0)
    owner_keys = jax.random.split(jax.random.fold_in(arg_keys[1], 1), TILES // TILES)
    owner_turns = jax.random.permutation(jax.random.fold_in(arg_keys[1], 3), TILES // TILES)
    owner = jax.vmap(lambda own, number: assign_block(jax.random.fold_in(arg_keys[1], 2), own, number, TILES, N_SHARD, 1, SLOT_DEV, 2))(owner_keys, owner_turns).reshape((TILES, 1))
    left_stat = draw_left_stat(jax.random.fold_in(arg_keys[7], 71), 0)
    right_stat = draw_right_stat(jax.random.fold_in(arg_keys[7], 71), 0)
    left_root = draw_left_root(jax.random.fold_in(arg_keys[7], 71), 0)
    right_root = draw_right_root(jax.random.fold_in(arg_keys[7], 71), 0)
    moment = jnp.clip(jnp.exp(math.log(10.0) - 4.6051702 * jax.random.uniform(arg_keys[6], (SLOTS, B, B), jnp.float32) ** block_levels(arg_keys[6], (SLOTS, B, B), ((0, 128),), -0.2, 0.2)), 0.1, 10.0)
    return {"grads": grads, "owner": owner, "left_stat": left_stat, "right_stat": right_stat, "left_root": left_root, "right_root": right_root, "moment": moment}


def positions(owner):
    owner_ids = owner[:, 0].astype(jnp.int32)
    tile_order = jnp.arange(owner_ids.shape[0], dtype=jnp.int32)
    earlier = (owner_ids[None, :] == owner_ids[:, None]) & (tile_order[None, :] < tile_order[:, None])
    slot_rank = lax.optimization_barrier(jnp.sum(earlier.astype(jnp.int32), axis=1)).astype(jnp.int32)
    return (owner_ids * SLOT_DEV + slot_rank).astype(jnp.int32)

def precondition(inputs):
    grad_tile, left_stat, right_stat, left_root, right_root, moment = inputs
    highest = lax.Precision.HIGHEST
    left_new = 0.95 * left_stat + jnp.dot(grad_tile, grad_tile.T, precision=highest, preferred_element_type=jnp.float32)
    right_new = 0.95 * right_stat + jnp.dot(grad_tile.T, grad_tile, precision=highest, preferred_element_type=jnp.float32)
    moment_new = 0.9 * moment + 0.1 * grad_tile * grad_tile
    adam_step = grad_tile / jnp.sqrt(moment_new)
    left_side = jnp.dot(left_root, grad_tile.astype(jnp.bfloat16), preferred_element_type=jnp.float32).astype(jnp.bfloat16)
    shaped = jnp.dot(left_side, right_root, preferred_element_type=jnp.float32)
    graft_ratio = jnp.sqrt(jnp.mean(adam_step * adam_step)) / jnp.sqrt(jnp.mean(shaped * shaped) + 1e-06)
    return (shaped * graft_ratio, left_new, right_new, moment_new)

def reference(grads, owner, left_stat, right_stat, left_root, right_root, moment):
    target = positions(owner)
    squares_all = jnp.sum(grads * grads)
    clip_scale = math.sqrt(TILES * B * B) / jnp.sqrt(squares_all)
    clipped = grads * clip_scale
    padded = jnp.zeros((SLOTS, B * B), jnp.float32).at[target].set(clipped)
    blocks = padded.reshape(SLOTS, B, B)
    scaled, left_new, right_new, moment_new = lax.map(precondition, (blocks, left_stat, right_stat, left_root, right_root, moment))
    update = scaled.reshape(SLOTS, B * B)[target]
    return (update, left_new, right_new, moment_new)
```

```python
import math

import jax
import jax.numpy as jnp
from jax import lax
from jax.sharding import PartitionSpec as P

B = 256
SLOT_DEV = 8


def positions(owner):
    owner_ids = owner[:, 0]
    tile_order = jnp.arange(owner_ids.shape[0], dtype=jnp.int32)
    earlier = (owner_ids[None, :] == owner_ids[:, None]) & (
        tile_order[None, :] < tile_order[:, None]
    )
    slot_rank = jnp.sum(earlier.astype(jnp.int32), axis=1)
    return owner_ids * SLOT_DEV + slot_rank


def total_over(value, axis_name, sizes):
    devices = lax.axis_size(axis_name)
    step = 1
    for size in sizes:
        block = step * size
        parts = [value]
        for shift in range(1, size):
            pairs = [
                (d, d // block * block + (d % block + shift * step) % block)
                for d in range(devices)
            ]
            parts.append(lax.ppermute(value, axis_name, pairs))
        value = sum(parts[1:], parts[0])
        step = block
    return value


def shards(grads, owner, left_stat, right_stat, left_root, right_root, moment):
    devices = lax.axis_size("shard")
    slot_count = left_stat.shape[0]
    shard_len = grads.shape[1]
    target = positions(owner)
    clip_limit = math.sqrt(grads.shape[0] * shard_len * devices)
    squares = jnp.sum(jnp.square(grads).reshape(-1, 8, 128), axis=0)
    outbox = jnp.zeros((devices * slot_count, shard_len), jnp.float32).at[target].set(grads)
    outbox = outbox.reshape(devices, slot_count, shard_len)
    arrived = lax.all_to_all(outbox, "shard", split_axis=0, concat_axis=2, tiled=True)
    squares_all = jnp.sum(total_over(squares, "shard", (2, 4, 4, 4)))
    clip_scale = clip_limit / jnp.sqrt(squares_all)
    blocks = arrived.reshape(slot_count, B, B) * clip_scale
    highest = lax.Precision.HIGHEST
    left_new = 0.95 * left_stat + jnp.einsum(
        "sij,skj->sik", blocks, blocks, precision=highest, preferred_element_type=jnp.float32
    )
    right_new = 0.95 * right_stat + jnp.einsum(
        "sji,sjk->sik", blocks, blocks, precision=highest, preferred_element_type=jnp.float32
    )
    moment_new = 0.9 * moment + 0.1 * blocks * blocks
    adam_step = blocks / jnp.sqrt(moment_new)
    left_side = jnp.einsum(
        "sij,sjk->sik", left_root, blocks.astype(jnp.bfloat16), preferred_element_type=jnp.float32
    ).astype(jnp.bfloat16)
    shaped = jnp.einsum("sij,sjk->sik", left_side, right_root, preferred_element_type=jnp.float32)
    graft_ratio = jnp.sqrt(jnp.mean(adam_step * adam_step, axis=(1, 2))) / jnp.sqrt(
        jnp.mean(shaped * shaped, axis=(1, 2)) + 1e-06
    )
    scaled = (shaped * graft_ratio[:, None, None]).reshape(slot_count, devices, shard_len)
    returned = lax.all_to_all(scaled, "shard", split_axis=1, concat_axis=0, tiled=True)
    gathered_rows = returned.reshape(devices * slot_count, shard_len)
    update = gathered_rows[target]
    return (update, left_new, right_new, moment_new)


def solution(mesh):
    return jax.shard_map(
        shards,
        mesh=mesh,
        in_specs=(
            P(None, "shard"),
            P(),
            P("shard", None, None),
            P("shard", None, None),
            P("shard", None, None),
            P("shard", None, None),
            P("shard", None, None),
        ),
        out_specs=(
            P(None, "shard"),
            P("shard", None, None),
            P("shard", None, None),
            P("shard", None, None),
        ),
        check_vma=False,
    )
```

```python
import functools
import math

import jax
import jax.numpy as jnp
from jax import lax
from jax.experimental import pallas as pl
from jax.experimental.pallas import tpu as pltpu
from jax.sharding import PartitionSpec as P

B = 256
SLOT_DEV = 8
LANES = 128
OUT_ROW = 2 * SLOT_DEV + 1
BACK_ROW = 2 * SLOT_DEV

ANY = pl.BlockSpec(memory_space=pl.ANY)
VMEM = pl.BlockSpec(memory_space=pltpu.VMEM)
SMEM = pl.BlockSpec(memory_space=pltpu.SMEM)
F32 = jnp.float32
BF16 = jnp.bfloat16


def call(kernel, in_specs, out_specs, out_shape, scratch, flops, bytes_accessed, vmem_mib=56):
    return pl.pallas_call(
        kernel,
        in_specs=in_specs,
        out_specs=out_specs,
        out_shape=out_shape,
        scratch_shapes=scratch,
        cost_estimate=pl.CostEstimate(flops=flops, bytes_accessed=bytes_accessed, transcendentals=0),
        compiler_params=pltpu.CompilerParams(vmem_limit_bytes=vmem_mib * 1024 * 1024),
    )


def started(source, target, sem):
    copy = pltpu.make_async_copy(source, target, sem)
    copy.start()
    return copy


def three_terms(x):
    high = x.astype(BF16)
    rest = x - high.astype(F32)
    middle = rest.astype(BF16)
    low = (rest - middle.astype(F32)).astype(BF16)
    return high, middle, low


def dot(a, b):
    return jnp.dot(a, b, preferred_element_type=F32)


def fold(x):
    total = jnp.sum(x.reshape(-1, 8, x.shape[1]), axis=0)
    return sum(total[:, lane : lane + LANES] for lane in range(0, x.shape[1], LANES))


def total_of(x):
    return jnp.sum(jnp.sum(x, axis=0, keepdims=True), axis=1, keepdims=True)


def pack_kernel(chunks, owner_hbm, grads_hbm, box, place_ref, owner, grads, sems):
    copies = [started(owner_hbm, owner, sems.at[0]), started(grads_hbm, grads, sems.at[1])]
    tiles = grads.shape[0]
    message = 2 * OUT_ROW
    copies[0].wait()
    owner_row = owner[...].astype(F32)
    owner_col = jnp.transpose(jnp.broadcast_to(owner_row, (8, tiles)))[:, :1]
    sub = lax.broadcasted_iota(jnp.int32, (tiles, tiles), 0)
    lane = lax.broadcasted_iota(jnp.int32, (tiles, tiles), 1)
    earlier = (owner_col == owner_row) & (sub < lane)
    rank = jnp.sum(earlier.astype(F32), axis=0, keepdims=True)
    place = rank * LANES + owner_row
    back = rank * 2 + owner_row * (2 * BACK_ROW)
    place_ref[...] = jnp.broadcast_to(back, (8, tiles)).astype(jnp.int32)
    copies[1].wait()
    squares = jnp.sum(fold(jnp.square(grads[...])), axis=0, keepdims=True)
    box[pl.ds(OUT_ROW - 1, LANES, stride=message), :] = jnp.broadcast_to(squares, (LANES, LANES))
    box[pl.ds(message - 1, LANES, stride=message), :] = jnp.zeros((LANES, LANES), F32)
    terms = jnp.concatenate(three_terms(grads[...]), axis=0)
    dests = LANES // chunks
    sub = lax.broadcasted_iota(jnp.int32, (SLOT_DEV * dests, tiles), 0)
    slots = (sub // dests * LANES + sub % dests).astype(F32)
    for k in range(chunks):
        chosen = (slots == place - float(k * dests)).astype(BF16)
        sent = dot(jnp.concatenate([chosen] * 3, axis=1), terms)
        for s in range(SLOT_DEV):
            for q in range(4):
                at = k * dests * message + q // 2 * OUT_ROW + 2 * s + q % 2
                box[pl.ds(at, dests, stride=message), :] = sent[
                    s * dests : (s + 1) * dests, q * LANES : (q + 1) * LANES
                ]


def clip_of(limit, box):
    squares = box[pl.ds(OUT_ROW - 1, LANES, stride=2 * OUT_ROW), :]
    return limit / jnp.sqrt(total_of(squares))


def tile_of(box, s):
    return jnp.concatenate([box[pl.ds(2 * s + c, B, stride=OUT_ROW), :] for c in range(2)], axis=1)


def shape_kernel(limit, chunks, box, left, right, moment, sent_hbm, shaped, sent, sems):
    clip = clip_of(limit, box)
    adam_sums, shaped_sums = [], []
    for s in range(SLOT_DEV):
        tile = tile_of(box, s) * clip
        half = dot(left[s], tile.astype(BF16)).astype(BF16)
        result = dot(half, right[s])
        shaped[s] = result
        square = tile * tile
        moment_new = 0.9 * moment[s] + 0.1 * square
        adam_sums.append(fold(square / moment_new))
        shaped_sums.append(fold(result * result))
    ratios = []
    for s in range(SLOT_DEV):
        adam_mean = total_of(adam_sums[s]) * (1.0 / (B * B))
        shaped_mean = total_of(shaped_sums[s]) * (1.0 / (B * B))
        ratios.append(jnp.sqrt(adam_mean) / jnp.sqrt(shaped_mean + 1e-06))
    rows = B // chunks
    out = []
    for k in range(chunks):
        for s in range(SLOT_DEV):
            result = shaped[s, k * rows : (k + 1) * rows, :] * ratios[s]
            for c in range(2):
                at = k * rows * BACK_ROW + 2 * s + c
                sent[pl.ds(at, rows, stride=BACK_ROW), :] = result[:, c * LANES : (c + 1) * LANES]
        part = pl.ds(k * rows * BACK_ROW, rows * BACK_ROW)
        out.append(started(sent.at[part], sent_hbm.at[part], sems.at[k]))
    for copy in out:
        copy.wait()


def stats_kernel(limit, box, left, right, moment, left_out, right_out, moment_out):
    clip = clip_of(limit, box)
    for s in range(SLOT_DEV):
        tile = tile_of(box, s) * clip
        moment_out[s] = 0.9 * moment[s] + 0.1 * (tile * tile)
        high = tile.astype(BF16)
        low = (tile - high.astype(F32)).astype(BF16)
        high_t, low_t = jnp.transpose(high), jnp.transpose(low)
        left_out[s] = 0.95 * left[s] + (dot(high, high_t) + (dot(high, low_t) + dot(low, high_t)))
        right_out[s] = 0.95 * right[s] + (dot(high_t, high) + (dot(high_t, low) + dot(low_t, high)))


def unpack_kernel(chunks, place, box, update_hbm, update, sems):
    groups = update.shape[0] // chunks
    out = []
    for k in range(chunks):

        def group(g, carry):
            for j in range(8):
                at = place[g * 8 + j]
                for q in range(4):
                    update[g, j : j + 1, q * LANES : (q + 1) * LANES] = box[
                        pl.ds(at + q // 2 * BACK_ROW + q % 2, 1), :
                    ]
            return carry

        lax.fori_loop(k * groups, (k + 1) * groups, group, 0)
        part = pl.ds(k * groups, groups)
        out.append(started(update.at[part], update_hbm.at[part], sems.at[k]))
    for copy in out:
        copy.wait()


def exchange(box):
    rows = box.reshape(box.shape[0], 1, LANES)
    rows = lax.all_to_all(rows, "shard", split_axis=0, concat_axis=0, tiled=True)
    return rows.reshape(box.shape)


def shards(grads, owner, left_stat, right_stat, left_root, right_root, moment):
    devices = lax.axis_size("shard")
    tiles, shard_len = grads.shape
    limit = math.sqrt(tiles * shard_len * devices)
    out_shape = jax.ShapeDtypeStruct((devices * 2 * OUT_ROW, LANES), F32)
    back_shape = jax.ShapeDtypeStruct((devices * 2 * BACK_ROW, LANES), F32)
    update_shape = jax.ShapeDtypeStruct((tiles // 8, 8, shard_len), F32)
    slots = left_stat.shape
    dma = pltpu.SemaphoreType.DMA

    outbox, place = call(
        functools.partial(pack_kernel, 4), [ANY, ANY], [VMEM, VMEM],
        [out_shape, jax.ShapeDtypeStruct((8, tiles), jnp.int32)],
        [pltpu.VMEM((1, tiles), jnp.int32), pltpu.VMEM(grads.shape, F32), dma((2,))],
        6 * tiles * devices * SLOT_DEV * shard_len, 16 * grads.size, 56,
    )(owner.reshape(1, tiles), grads)
    place = place[0]
    arrived = exchange(outbox)

    sent = call(
        functools.partial(shape_kernel, limit, 4), [VMEM] * 4, ANY, back_shape,
        [pltpu.VMEM(slots, F32), pltpu.VMEM(back_shape.shape, F32), dma((4,))],
        SLOT_DEV * 4 * B**3, SLOT_DEV * B * B * 16, 16,
    )(arrived, left_root, right_root, moment)
    returned = exchange(sent)

    left_new, right_new, moment_new = call(
        functools.partial(stats_kernel, limit), [VMEM] * 4, [VMEM] * 3, [jax.ShapeDtypeStruct(slots, F32)] * 3,
        [], SLOT_DEV * 12 * B**3, SLOT_DEV * B * B * 28, 32,
    )(arrived, left_stat, right_stat, moment)

    update = call(
        functools.partial(unpack_kernel, 3), [SMEM, VMEM], ANY, update_shape,
        [pltpu.VMEM(update_shape.shape, F32), dma((3,))], 2 * grads.size, 16 * grads.size, 8,
    )(place, returned)
    return (update.reshape(grads.shape), left_new, right_new, moment_new)


def solution(mesh):
    return jax.shard_map(
        shards,
        mesh=mesh,
        in_specs=(
            P(None, "shard"),
            P(),
            P("shard", None, None),
            P("shard", None, None),
            P("shard", None, None),
            P("shard", None, None),
            P("shard", None, None),
        ),
        out_specs=(
            P(None, "shard"),
            P("shard", None, None),
            P("shard", None, None),
            P("shard", None, None),
        ),
        check_vma=False,
    )
```

```python
import functools
import math

import jax
import jax.numpy as jnp
from jax import lax
from jax.experimental import pallas as pl
from jax.experimental.pallas import tpu as pltpu
from jax.sharding import PartitionSpec as P

B = 256
SLOT_DEV = 8
LANES = 128
OUT_ROW = 2 * SLOT_DEV + 1
BACK_ROW = 2 * SLOT_DEV

HBM = pl.BlockSpec(memory_space=pltpu.HBM)
VMEM = pl.BlockSpec(memory_space=pltpu.VMEM)
SMEM = pl.BlockSpec(memory_space=pltpu.SMEM)
F32 = jnp.float32
BF16 = jnp.bfloat16


def call(kernel, in_specs, out_specs, out_shape, scratch, flops, bytes_accessed, vmem_mib=56):
    return pl.pallas_call(
        kernel,
        in_specs=in_specs,
        out_specs=out_specs,
        out_shape=out_shape,
        scratch_shapes=scratch,
        cost_estimate=pl.CostEstimate(flops=flops, bytes_accessed=bytes_accessed, transcendentals=0),
        compiler_params=pltpu.CompilerParams(vmem_limit_bytes=vmem_mib * 1024 * 1024),
    )


def started(source, target, sem):
    copy = pltpu.make_async_copy(source, target, sem)
    copy.start()
    return copy


def two_terms(x):
    high = x.astype(BF16)
    return high, (x - high.astype(F32)).astype(BF16)


def dot(a, b):
    return jnp.dot(a, b, preferred_element_type=F32)


def fold(x):
    total = jnp.sum(x.reshape(-1, 8, x.shape[1]), axis=0)
    return sum(total[:, lane : lane + LANES] for lane in range(0, x.shape[1], LANES))


def total_of(x):
    return jnp.sum(jnp.sum(x, axis=0, keepdims=True), axis=1, keepdims=True)


def pack_kernel(chunks, owner_hbm, grads_hbm, box, place_ref, owner, grads, chosen, sems):
    copies = [started(owner_hbm, owner, sems.at[0]), started(grads_hbm, grads, sems.at[1])]
    tiles = grads.shape[0]
    message = 2 * OUT_ROW
    sub = lax.broadcasted_iota(jnp.int32, (tiles, tiles), 0)
    lane = lax.broadcasted_iota(jnp.int32, (tiles, tiles), 1)
    box[pl.ds(message - 1, LANES, stride=message), :] = jnp.zeros((LANES, LANES), F32)
    copies[0].wait()
    owner_row = owner[...].astype(F32)
    owner_col = jnp.transpose(jnp.broadcast_to(owner_row, (8, tiles)))[:, :1]
    earlier = (owner_col == owner_row) & (sub < lane)
    rank = jnp.sum(earlier.astype(F32), axis=0, keepdims=True)
    back = rank * 2 + owner_row * (2 * BACK_ROW)
    place_ref[...] = jnp.broadcast_to(back, (8, tiles)).astype(jnp.int32)
    dests = LANES // chunks
    rows = SLOT_DEV * dests
    sub = lax.broadcasted_iota(jnp.int32, (dests, tiles), 0).astype(F32)
    for k in range(chunks):
        mine = sub == owner_row - float(k * dests)
        for s in range(SLOT_DEV):
            at = k * rows + s * dests
            chosen[at : at + dests, :] = (mine & (rank == float(s))).astype(BF16)
    copies[1].wait()
    squares = jnp.sum(fold(jnp.square(grads[...])), axis=0, keepdims=True)
    box[pl.ds(OUT_ROW - 1, LANES, stride=message), :] = jnp.broadcast_to(squares, (LANES, LANES))
    terms = two_terms(grads[...])
    for k in range(chunks):
        taken = chosen[k * rows : (k + 1) * rows, :]
        sent = dot(taken, terms[0]) + dot(taken, terms[1])
        for s in range(SLOT_DEV):
            for q in range(4):
                at = k * dests * message + q // 2 * OUT_ROW + 2 * s + q % 2
                box[pl.ds(at, dests, stride=message), :] = sent[
                    s * dests : (s + 1) * dests, q * LANES : (q + 1) * LANES
                ]


def clip_of(limit, box):
    squares = box[pl.ds(OUT_ROW - 1, LANES, stride=2 * OUT_ROW), :]
    return limit / jnp.sqrt(total_of(squares))


def tile_of(box, s):
    return jnp.concatenate([box[pl.ds(2 * s + c, B, stride=OUT_ROW), :] for c in range(2)], axis=1)


def shape_kernel(limit, chunks, box, left, right, moment, sent_hbm, shaped, sent, sems):
    clip = clip_of(limit, box)
    adam_sums, shaped_sums = [], []
    for s in range(SLOT_DEV):
        tile = tile_of(box, s) * clip
        half = dot(left[s], tile.astype(BF16)).astype(BF16)
        result = dot(half, right[s])
        shaped[s] = result
        square = tile * tile
        moment_new = 0.9 * moment[s] + 0.1 * square
        adam_sums.append(fold(square / moment_new))
        shaped_sums.append(fold(result * result))
    ratios = []
    for s in range(SLOT_DEV):
        adam_mean = total_of(adam_sums[s]) * (1.0 / (B * B))
        shaped_mean = total_of(shaped_sums[s]) * (1.0 / (B * B))
        ratios.append(jnp.sqrt(adam_mean) / jnp.sqrt(shaped_mean + 1e-06))
    rows = B // chunks
    out = []
    for k in range(chunks):
        for s in range(SLOT_DEV):
            result = shaped[s, k * rows : (k + 1) * rows, :] * ratios[s]
            for c in range(2):
                at = k * rows * BACK_ROW + 2 * s + c
                sent[pl.ds(at, rows, stride=BACK_ROW), :] = result[:, c * LANES : (c + 1) * LANES]
        part = pl.ds(k * rows * BACK_ROW, rows * BACK_ROW)
        out.append(started(sent.at[part], sent_hbm.at[part], sems.at[k]))
    for copy in out:
        copy.wait()


def stats_kernel(limit, box, left, right, moment, left_out, right_out, moment_out):
    clip = clip_of(limit, box)
    for s in range(SLOT_DEV):
        tile = tile_of(box, s) * clip
        moment_out[s] = 0.9 * moment[s] + 0.1 * (tile * tile)
        high = tile.astype(BF16)
        low = (tile - high.astype(F32)).astype(BF16)
        high_t, low_t = jnp.transpose(high), jnp.transpose(low)
        left_out[s] = 0.95 * left[s] + (dot(high, high_t) + (dot(high, low_t) + dot(low, high_t)))
        right_out[s] = 0.95 * right[s] + (dot(high_t, high) + (dot(high_t, low) + dot(low_t, high)))


def unpack_kernel(chunks, place, box, update_hbm, update, sems):
    groups = update.shape[0] // chunks
    out = []
    for k in range(chunks):

        def group(g, carry):
            for j in range(8):
                at = place[g * 8 + j]
                for q in range(4):
                    update[g, j : j + 1, q * LANES : (q + 1) * LANES] = box[
                        pl.ds(at + q // 2 * BACK_ROW + q % 2, 1), :
                    ]
            return carry

        lax.fori_loop(k * groups, (k + 1) * groups, group, 0)
        part = pl.ds(k * groups, groups)
        out.append(started(update.at[part], update_hbm.at[part], sems.at[k]))
    for copy in out:
        copy.wait()


def exchange(box):
    rows = box.reshape(box.shape[0], 1, LANES)
    rows = lax.all_to_all(rows, "shard", split_axis=0, concat_axis=0, tiled=True)
    return rows.reshape(box.shape)


def shards(grads, owner, left_stat, right_stat, left_root, right_root, moment):
    devices = lax.axis_size("shard")
    tiles, shard_len = grads.shape
    limit = math.sqrt(tiles * shard_len * devices)
    out_shape = (devices * 2 * OUT_ROW, LANES)
    back_shape = (devices * 2 * BACK_ROW, LANES)
    update_shape = (tiles // 8, 8, shard_len)
    in_hbm = functools.partial(pltpu.with_memory_space_constraint, memory_space=pltpu.HBM)
    in_vmem = functools.partial(pltpu.with_memory_space_constraint, memory_space=pltpu.VMEM)
    slots = left_stat.shape
    dma = pltpu.SemaphoreType.DMA

    outbox, place = call(
        functools.partial(pack_kernel, 2), [HBM, HBM], [VMEM, VMEM],
        [pltpu.VMEM(out_shape, F32), jax.ShapeDtypeStruct((8, tiles), jnp.int32)],
        [pltpu.VMEM((1, tiles), jnp.int32), pltpu.VMEM(grads.shape, F32),
         pltpu.VMEM((devices * SLOT_DEV, tiles), BF16), dma((2,))],
        4 * tiles * devices * SLOT_DEV * shard_len, 16 * grads.size, 16,
    )(in_hbm(owner.reshape(1, tiles)), in_hbm(grads))
    place = place[0]
    arrived = exchange(outbox)

    sent = call(
        functools.partial(shape_kernel, limit, 4), [VMEM] * 4, HBM, pltpu.HBM(back_shape, F32),
        [pltpu.VMEM(slots, F32), pltpu.VMEM(back_shape, F32), dma((4,))],
        SLOT_DEV * 4 * B**3, SLOT_DEV * B * B * 16, 16,
    )(arrived, left_root, right_root, moment)
    returned = lax.all_to_all(sent, "shard", split_axis=0, concat_axis=0, tiled=True)

    left_new, right_new, moment_new = call(
        functools.partial(stats_kernel, limit), [VMEM] * 4, [VMEM] * 3, [jax.ShapeDtypeStruct(slots, F32)] * 3,
        [], SLOT_DEV * 12 * B**3, SLOT_DEV * B * B * 28, 20,
    )(arrived, left_stat, right_stat, moment)

    update = call(
        functools.partial(unpack_kernel, 3), [SMEM, VMEM], HBM, jax.ShapeDtypeStruct(update_shape, F32),
        [pltpu.VMEM(update_shape, F32), dma((3,))], 2 * grads.size, 16 * grads.size, 8,
    )(place, in_vmem(returned))
    return (update.reshape(grads.shape), left_new, right_new, moment_new)


def solution(mesh):
    return jax.shard_map(
        shards,
        mesh=mesh,
        in_specs=(
            P(None, "shard"),
            P(),
            P("shard", None, None),
            P("shard", None, None),
            P("shard", None, None),
            P("shard", None, None),
            P("shard", None, None),
        ),
        out_specs=(
            P(None, "shard"),
            P("shard", None, None),
            P("shard", None, None),
            P("shard", None, None),
        ),
        check_vma=False,
    )
```

```python
import functools
import math

import jax
import jax.numpy as jnp
from jax import lax
from jax.experimental import pallas as pl
from jax.experimental.pallas import tpu as pltpu
from jax.sharding import PartitionSpec as P

B = 256
SLOT_DEV = 8
LANES = 128
OUT_ROW = 2 * SLOT_DEV + 1
BACK_ROW = 2 * SLOT_DEV

HBM = pl.BlockSpec(memory_space=pltpu.HBM)
VMEM = pl.BlockSpec(memory_space=pltpu.VMEM)
SMEM = pl.BlockSpec(memory_space=pltpu.SMEM)
F32 = jnp.float32
BF16 = jnp.bfloat16


def call(kernel, in_specs, out_specs, out_shape, scratch, flops, bytes_accessed, vmem_mib=56):
    return pl.pallas_call(
        kernel,
        in_specs=in_specs,
        out_specs=out_specs,
        out_shape=out_shape,
        scratch_shapes=scratch,
        cost_estimate=pl.CostEstimate(flops=flops, bytes_accessed=bytes_accessed, transcendentals=0),
        compiler_params=pltpu.CompilerParams(vmem_limit_bytes=vmem_mib * 1024 * 1024),
    )


def started(source, target, sem):
    copy = pltpu.make_async_copy(source, target, sem)
    copy.start()
    return copy


def two_terms(x):
    high = x.astype(BF16)
    return high, (x - high.astype(F32)).astype(BF16)


def dot(a, b):
    return jnp.dot(a, b, preferred_element_type=F32)


def fold(x):
    total = jnp.sum(x.reshape(-1, 8, x.shape[1]), axis=0)
    return sum(total[:, lane : lane + LANES] for lane in range(0, x.shape[1], LANES))


def total_of(x):
    return jnp.sum(jnp.sum(x, axis=0, keepdims=True), axis=1, keepdims=True)


def pack_kernel(chunks, owner_hbm, grads_hbm, box, place_ref, owner, grads, chosen, sems):
    copies = [started(owner_hbm, owner, sems.at[0]), started(grads_hbm, grads, sems.at[1])]
    tiles = grads.shape[0]
    message = 2 * OUT_ROW
    sub = lax.broadcasted_iota(jnp.int32, (tiles, tiles), 0)
    lane = lax.broadcasted_iota(jnp.int32, (tiles, tiles), 1)
    box[pl.ds(message - 1, LANES, stride=message), :] = jnp.zeros((LANES, LANES), F32)
    copies[0].wait()
    owner_row = owner[...].astype(F32)
    owner_col = jnp.transpose(jnp.broadcast_to(owner_row, (8, tiles)))[:, :1]
    earlier = (owner_col == owner_row) & (sub < lane)
    rank = jnp.sum(earlier.astype(F32), axis=0, keepdims=True)
    back = rank * 2 + owner_row * (2 * BACK_ROW)
    place_ref[...] = jnp.broadcast_to(back, (8, tiles)).astype(jnp.int32)
    dests = LANES // chunks
    rows = SLOT_DEV * dests
    sub = lax.broadcasted_iota(jnp.int32, (dests, tiles), 0).astype(F32)
    for k in range(chunks):
        mine = sub == owner_row - float(k * dests)
        for s in range(SLOT_DEV):
            at = k * rows + s * dests
            chosen[at : at + dests, :] = (mine & (rank == float(s))).astype(BF16)
    copies[1].wait()
    squares = jnp.sum(fold(jnp.square(grads[...])), axis=0, keepdims=True)
    box[pl.ds(OUT_ROW - 1, LANES, stride=message), :] = jnp.broadcast_to(squares, (LANES, LANES))
    terms = jnp.concatenate(two_terms(grads[...]), axis=0)
    for k in range(chunks):
        taken = chosen[k * rows : (k + 1) * rows, :]
        sent = dot(jnp.concatenate([taken, taken], axis=1), terms)
        for s in range(SLOT_DEV):
            for q in range(4):
                at = k * dests * message + q // 2 * OUT_ROW + 2 * s + q % 2
                box[pl.ds(at, dests, stride=message), :] = sent[
                    s * dests : (s + 1) * dests, q * LANES : (q + 1) * LANES
                ]


def clip_of(limit, box):
    squares = box[pl.ds(OUT_ROW - 1, LANES, stride=2 * OUT_ROW), :]
    return limit / jnp.sqrt(total_of(squares))


def tile_of(box, s):
    return jnp.concatenate([box[pl.ds(2 * s + c, B, stride=OUT_ROW), :] for c in range(2)], axis=1)


def shape_kernel(limit, chunks, box, left, right, moment, sent_hbm, shaped, sent, sems):
    clip = clip_of(limit, box)
    adam_sums, shaped_sums = [], []
    for s in range(SLOT_DEV):
        tile = tile_of(box, s) * clip
        half = dot(left[s], tile.astype(BF16)).astype(BF16)
        result = dot(half, right[s])
        shaped[s] = result
        square = tile * tile
        moment_new = 0.9 * moment[s] + 0.1 * square
        adam_sums.append(fold(square / moment_new))
        shaped_sums.append(fold(result * result))
    ratios = []
    for s in range(SLOT_DEV):
        adam_mean = total_of(adam_sums[s]) * (1.0 / (B * B))
        shaped_mean = total_of(shaped_sums[s]) * (1.0 / (B * B))
        ratios.append(jnp.sqrt(adam_mean) / jnp.sqrt(shaped_mean + 1e-06))
    rows = B // chunks
    out = []
    for k in range(chunks):
        for s in range(SLOT_DEV):
            result = shaped[s, k * rows : (k + 1) * rows, :] * ratios[s]
            for c in range(2):
                at = k * rows * BACK_ROW + 2 * s + c
                sent[pl.ds(at, rows, stride=BACK_ROW), :] = result[:, c * LANES : (c + 1) * LANES]
        part = pl.ds(k * rows * BACK_ROW, rows * BACK_ROW)
        out.append(started(sent.at[part], sent_hbm.at[part], sems.at[k]))
    for copy in out:
        copy.wait()


def stats_kernel(limit, box, left, right, moment, left_out, right_out, moment_out):
    clip = clip_of(limit, box)
    s = pl.program_id(0)
    tile = jnp.concatenate([box[pl.ds(2 * s + c, B, stride=OUT_ROW), :] for c in range(2)], axis=1) * clip
    moment_out[0] = 0.9 * moment[0] + 0.1 * (tile * tile)
    high = tile.astype(BF16)
    low = (tile - high.astype(F32)).astype(BF16)
    high_t, low_t = jnp.transpose(high), jnp.transpose(low)
    left_out[0] = 0.95 * left[0] + (dot(high, high_t) + (dot(high, low_t) + dot(low, high_t)))
    right_out[0] = 0.95 * right[0] + (dot(high_t, high) + (dot(high_t, low) + dot(low_t, high)))


def unpack_kernel(chunks, place, box, update_hbm, update, sems):
    groups = update.shape[0] // chunks
    out = []
    for k in range(chunks):

        def group(g, carry):
            for j in range(8):
                at = place[g * 8 + j]
                for q in range(4):
                    update[g, j : j + 1, q * LANES : (q + 1) * LANES] = box[
                        pl.ds(at + q // 2 * BACK_ROW + q % 2, 1), :
                    ]
            return carry

        lax.fori_loop(k * groups, (k + 1) * groups, group, 0)
        part = pl.ds(k * groups, groups)
        out.append(started(update.at[part], update_hbm.at[part], sems.at[k]))
    for copy in out:
        copy.wait()


def exchange(box):
    rows = box.reshape(box.shape[0], 1, LANES)
    rows = lax.all_to_all(rows, "shard", split_axis=0, concat_axis=0, tiled=True)
    return rows.reshape(box.shape)


def shards(grads, owner, left_stat, right_stat, left_root, right_root, moment):
    devices = lax.axis_size("shard")
    tiles, shard_len = grads.shape
    limit = math.sqrt(tiles * shard_len * devices)
    out_shape = (devices * 2 * OUT_ROW, LANES)
    back_shape = (devices * 2 * BACK_ROW, LANES)
    update_shape = (tiles // 8, 8, shard_len)
    in_hbm = functools.partial(pltpu.with_memory_space_constraint, memory_space=pltpu.HBM)
    in_vmem = functools.partial(pltpu.with_memory_space_constraint, memory_space=pltpu.VMEM)
    slots = left_stat.shape
    dma = pltpu.SemaphoreType.DMA

    outbox, place = call(
        functools.partial(pack_kernel, 2), [HBM, HBM], [VMEM, VMEM],
        [pltpu.VMEM(out_shape, F32), jax.ShapeDtypeStruct((8, tiles), jnp.int32)],
        [pltpu.VMEM((1, tiles), jnp.int32), pltpu.VMEM(grads.shape, F32),
         pltpu.VMEM((devices * SLOT_DEV, tiles), BF16), dma((2,))],
        4 * tiles * devices * SLOT_DEV * shard_len, 16 * grads.size, 16,
    )(in_hbm(owner.reshape(1, tiles)), in_hbm(grads))
    place = place[0]
    arrived = exchange(outbox)

    sent = call(
        functools.partial(shape_kernel, limit, 8), [VMEM] * 4, HBM, pltpu.HBM(back_shape, F32),
        [pltpu.VMEM(slots, F32), pltpu.VMEM(back_shape, F32), dma((8,))],
        SLOT_DEV * 4 * B**3, SLOT_DEV * B * B * 16, 16,
    )(arrived, left_root, right_root, moment)
    returned = lax.all_to_all(sent, "shard", split_axis=0, concat_axis=0, tiled=True)

    slot = pl.BlockSpec((1, B, B), lambda s: (s, 0, 0))
    left_new, right_new, moment_new = pl.pallas_call(
        functools.partial(stats_kernel, limit),
        grid=(SLOT_DEV,),
        in_specs=[VMEM] + [slot] * 3,
        out_specs=[slot] * 3,
        out_shape=[pltpu.HBM(slots, F32)] * 3,
        cost_estimate=pl.CostEstimate(flops=SLOT_DEV * 12 * B**3, bytes_accessed=SLOT_DEV * B * B * 28, transcendentals=0),
        compiler_params=pltpu.CompilerParams(vmem_limit_bytes=8 * 1024 * 1024),
    )(in_hbm(arrived), in_hbm(left_stat), in_hbm(right_stat), in_hbm(moment))

    update = call(
        functools.partial(unpack_kernel, 3), [SMEM, VMEM], HBM, jax.ShapeDtypeStruct(update_shape, F32),
        [pltpu.VMEM(update_shape, F32), dma((3,))], 2 * grads.size, 16 * grads.size, 8,
    )(place, in_vmem(returned))
    return (update.reshape(grads.shape), left_new, right_new, moment_new)


def solution(mesh):
    return jax.shard_map(
        shards,
        mesh=mesh,
        in_specs=(
            P(None, "shard"),
            P(),
            P("shard", None, None),
            P("shard", None, None),
            P("shard", None, None),
            P("shard", None, None),
            P("shard", None, None),
        ),
        out_specs=(
            P(None, "shard"),
            P("shard", None, None),
            P("shard", None, None),
            P("shard", None, None),
        ),
        check_vma=False,
    )
```

```python
import functools
import math

import jax
import jax.numpy as jnp
from jax import lax
from jax.experimental import pallas as pl
from jax.experimental.pallas import tpu as pltpu
from jax.sharding import PartitionSpec as P

B = 256
SLOT_DEV = 8
LANES = 128
OUT_ROW = 2 * SLOT_DEV
OUT_MESSAGE = 2 * OUT_ROW + 1
BACK_ROW = 2 * SLOT_DEV

HBM = pl.BlockSpec(memory_space=pltpu.HBM)
VMEM = pl.BlockSpec(memory_space=pltpu.VMEM)
SMEM = pl.BlockSpec(memory_space=pltpu.SMEM)
F32 = jnp.float32
BF16 = jnp.bfloat16


def call(kernel, in_specs, out_specs, out_shape, scratch, flops, bytes_accessed, vmem_mib=56):
    return pl.pallas_call(
        kernel,
        in_specs=in_specs,
        out_specs=out_specs,
        out_shape=out_shape,
        scratch_shapes=scratch,
        cost_estimate=pl.CostEstimate(flops=flops, bytes_accessed=bytes_accessed, transcendentals=0),
        compiler_params=pltpu.CompilerParams(vmem_limit_bytes=vmem_mib * 1024 * 1024),
    )


def started(source, target, sem):
    copy = pltpu.make_async_copy(source, target, sem)
    copy.start()
    return copy


def two_terms(x):
    high = x.astype(BF16)
    return high, (x - high.astype(F32)).astype(BF16)


def dot(a, b):
    return jnp.dot(a, b, preferred_element_type=F32)


def fold(x):
    total = jnp.sum(x.reshape(-1, 8, x.shape[1]), axis=0)
    return sum(total[:, lane : lane + LANES] for lane in range(0, x.shape[1], LANES))


def total_of(x):
    return jnp.sum(jnp.sum(x, axis=0, keepdims=True), axis=1, keepdims=True)


def pack_kernel(chunks, owner_hbm, grads_hbm, box, place_ref, owner, grads, chosen, sems):
    copies = [started(owner_hbm, owner, sems.at[0]), started(grads_hbm, grads, sems.at[1])]
    tiles = grads.shape[0]
    message = OUT_MESSAGE
    sub = lax.broadcasted_iota(jnp.int32, (tiles, tiles), 0)
    lane = lax.broadcasted_iota(jnp.int32, (tiles, tiles), 1)
    copies[0].wait()
    owner_row = owner[...].astype(F32)
    owner_col = jnp.transpose(jnp.broadcast_to(owner_row, (8, tiles)))[:, :1]
    earlier = (owner_col == owner_row) & (sub < lane)
    rank = jnp.sum(earlier.astype(F32), axis=0, keepdims=True)
    back = rank * 2 + owner_row * (2 * BACK_ROW)
    place_ref[...] = jnp.broadcast_to(back, (8, tiles)).astype(jnp.int32)
    dests = LANES // chunks
    rows = SLOT_DEV * dests
    sub = lax.broadcasted_iota(jnp.int32, (dests, tiles), 0).astype(F32)
    for k in range(chunks):
        mine = sub == owner_row - float(k * dests)
        for s in range(SLOT_DEV):
            at = k * rows + s * dests
            chosen[at : at + dests, :] = (mine & (rank == float(s))).astype(BF16)
    copies[1].wait()
    squares = jnp.sum(fold(jnp.square(grads[...])), axis=0, keepdims=True)
    box[pl.ds(message - 1, LANES, stride=message), :] = jnp.broadcast_to(squares, (LANES, LANES))
    terms = jnp.concatenate(two_terms(grads[...]), axis=0)
    for k in range(chunks):
        taken = chosen[k * rows : (k + 1) * rows, :]
        sent = dot(jnp.concatenate([taken, taken], axis=1), terms)
        for s in range(SLOT_DEV):
            for q in range(4):
                at = k * dests * message + q // 2 * OUT_ROW + 2 * s + q % 2
                box[pl.ds(at, dests, stride=message), :] = sent[
                    s * dests : (s + 1) * dests, q * LANES : (q + 1) * LANES
                ]


def clip_of(limit, box):
    squares = box[pl.ds(OUT_MESSAGE - 1, LANES, stride=OUT_MESSAGE), :]
    return limit / jnp.sqrt(total_of(squares))


def tile_of(box, s, clip, rows):
    for c in range(2):
        for parity in range(2):
            at = parity * OUT_ROW + 2 * s + c
            rows[c, pl.ds(parity, LANES, stride=2), :] = box[pl.ds(at, LANES, stride=OUT_MESSAGE), :] * clip
    return jnp.concatenate([rows[0], rows[1]], axis=1)


def shape_kernel(limit, chunks, box, left, right, moment, sent_hbm, ordered, sent, sems):
    clip = clip_of(limit, box)
    rows_of = sent.reshape(B, BACK_ROW, LANES)
    sums, out = [], []

    def send(half, pieces):
        ratios = []
        for adam_sum, shaped_sum in sums[4 * half : 4 * half + 4]:
            adam_mean = total_of(adam_sum) * (1.0 / (B * B))
            shaped_mean = total_of(shaped_sum) * (1.0 / (B * B))
            ratio = jnp.sqrt(adam_mean) / jnp.sqrt(shaped_mean + 1e-06)
            ratios.append(jnp.broadcast_to(ratio, (2, LANES)))
        ratios = jnp.concatenate(ratios, axis=0)
        rows = B // pieces
        for k in range(pieces):
            part = (pl.ds(k * rows, rows), pl.ds(8 * half, 8))
            rows_of[part] = rows_of[part] * ratios
            out.append(started(rows_of.at[part], sent_hbm.at[part], sems.at[len(out)]))

    for s in range(SLOT_DEV):
        tile = tile_of(box, s, clip, ordered.at[s])
        half = dot(left[s], tile.astype(BF16)).astype(BF16)
        shaped = dot(half, right[s])
        for c in range(2):
            sent[pl.ds(2 * s + c, B, stride=BACK_ROW), :] = shaped[:, c * LANES : (c + 1) * LANES]
        square = tile * tile
        moment_new = 0.9 * moment[s] + 0.1 * square
        sums.append((fold(square / moment_new), fold(shaped * shaped)))
        if s == 4:
            send(0, chunks[0])
    send(1, chunks[1])
    for copy in out:
        copy.wait()


def stats_kernel(limit, box, left, right, moment, left_out, right_out, moment_out, ordered):
    clip = clip_of(limit, box)
    s = pl.program_id(0)
    tile = tile_of(box, s, clip, ordered)
    moment_out[0] = 0.9 * moment[0] + 0.1 * (tile * tile)
    high = tile.astype(BF16)
    low = (tile - high.astype(F32)).astype(BF16)
    high_t, low_t = jnp.transpose(high), jnp.transpose(low)
    left_out[0] = 0.95 * left[0] + (dot(high, high_t) + (dot(high, low_t) + dot(low, high_t)))
    right_out[0] = 0.95 * right[0] + (dot(high_t, high) + (dot(high_t, low) + dot(low_t, high)))


def unpack_kernel(chunks, place, box, update_hbm, update, sems):
    groups = update.shape[0] // chunks
    unroll = 2
    out = []
    for k in range(chunks):

        def group(step, carry):
            for g in range(unroll):
                for j in range(8):
                    at = place[(step * unroll + g) * 8 + j]
                    for q in range(4):
                        update[step * unroll + g, j : j + 1, q * LANES : (q + 1) * LANES] = box[
                            pl.ds(at + q // 2 * BACK_ROW + q % 2, 1), :
                        ]
            return carry

        lax.fori_loop(k * groups // unroll, (k + 1) * groups // unroll, group, 0)
        part = pl.ds(k * groups, groups)
        out.append(started(update.at[part], update_hbm.at[part], sems.at[k]))
    for copy in out:
        copy.wait()


def exchange(box):
    rows = box.reshape(box.shape[0], 1, LANES)
    rows = lax.all_to_all(rows, "shard", split_axis=0, concat_axis=0, tiled=True)
    return rows.reshape(box.shape)


def shards(grads, owner, left_stat, right_stat, left_root, right_root, moment):
    devices = lax.axis_size("shard")
    tiles, shard_len = grads.shape
    limit = math.sqrt(tiles * shard_len * devices)
    out_shape = (devices * OUT_MESSAGE, LANES)
    back_shape = (devices * 2 * BACK_ROW, LANES)
    update_shape = (tiles // 8, 8, shard_len)
    in_hbm = functools.partial(pltpu.with_memory_space_constraint, memory_space=pltpu.HBM)
    in_vmem = functools.partial(pltpu.with_memory_space_constraint, memory_space=pltpu.VMEM)
    slots = left_stat.shape
    dma = pltpu.SemaphoreType.DMA

    outbox, place = call(
        functools.partial(pack_kernel, 2), [HBM, HBM], [VMEM, VMEM],
        [pltpu.VMEM(out_shape, F32), jax.ShapeDtypeStruct((8, tiles), jnp.int32)],
        [pltpu.VMEM((1, tiles), jnp.int32), pltpu.VMEM(grads.shape, F32),
         pltpu.VMEM((devices * SLOT_DEV, tiles), BF16), dma((2,))],
        4 * tiles * devices * SLOT_DEV * shard_len, 16 * grads.size, 16,
    )(in_hbm(owner.reshape(1, tiles)), in_hbm(grads))
    place = place[0]
    arrived = exchange(outbox)

    sent = call(
        functools.partial(shape_kernel, limit, (2, 8)), [VMEM] * 4, HBM, pltpu.HBM((B, BACK_ROW, LANES), F32),
        [pltpu.VMEM((SLOT_DEV, 2, B, LANES), F32), pltpu.VMEM(back_shape, F32), dma((10,))],
        SLOT_DEV * 4 * B**3, SLOT_DEV * B * B * 16, 16,
    )(arrived, left_root, right_root, moment)
    returned = lax.all_to_all(sent.reshape(back_shape), "shard", split_axis=0, concat_axis=0, tiled=True)

    slot = pl.BlockSpec((1, B, B), lambda s: (s, 0, 0))
    left_new, right_new, moment_new = pl.pallas_call(
        functools.partial(stats_kernel, limit),
        grid=(SLOT_DEV,),
        in_specs=[VMEM] + [slot] * 3,
        out_specs=[slot] * 3,
        out_shape=[pltpu.HBM(slots, F32)] * 3,
        scratch_shapes=[pltpu.VMEM((2, B, LANES), F32)],
        cost_estimate=pl.CostEstimate(flops=SLOT_DEV * 12 * B**3, bytes_accessed=SLOT_DEV * B * B * 28, transcendentals=0),
        compiler_params=pltpu.CompilerParams(vmem_limit_bytes=8 * 1024 * 1024),
    )(in_hbm(arrived), in_hbm(left_stat), in_hbm(right_stat), in_hbm(moment))

    update = call(
        functools.partial(unpack_kernel, 3), [SMEM, VMEM], HBM, jax.ShapeDtypeStruct(update_shape, F32),
        [pltpu.VMEM(update_shape, F32), dma((3,))], 2 * grads.size, 16 * grads.size, 8,
    )(place, in_vmem(returned))
    return (update.reshape(grads.shape), left_new, right_new, moment_new)


def solution(mesh):
    return jax.shard_map(
        shards,
        mesh=mesh,
        in_specs=(
            P(None, "shard"),
            P(),
            P("shard", None, None),
            P("shard", None, None),
            P("shard", None, None),
            P("shard", None, None),
            P("shard", None, None),
        ),
        out_specs=(
            P(None, "shard"),
            P("shard", None, None),
            P("shard", None, None),
            P("shard", None, None),
        ),
        check_vma=False,
    )
```

```python
import functools
import math

import jax
import jax.numpy as jnp
from jax import lax
from jax.experimental import pallas as pl
from jax.experimental.pallas import tpu as pltpu
from jax.sharding import PartitionSpec as P

B = 256
SLOT_DEV = 8
LANES = 128
OUT_ROW = 2 * SLOT_DEV
OUT_MESSAGE = 2 * OUT_ROW + 1
BACK_ROW = 2 * SLOT_DEV

HBM = pl.BlockSpec(memory_space=pltpu.HBM)
VMEM = pl.BlockSpec(memory_space=pltpu.VMEM)
SMEM = pl.BlockSpec(memory_space=pltpu.SMEM)
F32 = jnp.float32
BF16 = jnp.bfloat16


def call(kernel, in_specs, out_specs, out_shape, scratch, flops, bytes_accessed, vmem_mib=56):
    return pl.pallas_call(
        kernel,
        in_specs=in_specs,
        out_specs=out_specs,
        out_shape=out_shape,
        scratch_shapes=scratch,
        cost_estimate=pl.CostEstimate(flops=flops, bytes_accessed=bytes_accessed, transcendentals=0),
        compiler_params=pltpu.CompilerParams(vmem_limit_bytes=vmem_mib * 1024 * 1024),
    )


def started(source, target, sem):
    copy = pltpu.make_async_copy(source, target, sem)
    copy.start()
    return copy


def two_terms(x):
    high = x.astype(BF16)
    return high, (x - high.astype(F32)).astype(BF16)


def dot(a, b):
    return jnp.dot(a, b, preferred_element_type=F32)


def fold(x):
    total = jnp.sum(x.reshape(-1, 8, x.shape[1]), axis=0)
    return sum(total[:, lane : lane + LANES] for lane in range(0, x.shape[1], LANES))


def total_of(x):
    return jnp.sum(jnp.sum(x, axis=0, keepdims=True), axis=1, keepdims=True)


def pack_kernel(chunks, owner_hbm, grads_hbm, box, place_ref, owner, grads, chosen, sems):
    copies = [started(owner_hbm, owner, sems.at[0]), started(grads_hbm, grads, sems.at[1])]
    tiles = grads.shape[0]
    message = OUT_MESSAGE
    sub = lax.broadcasted_iota(jnp.int32, (tiles, tiles), 0)
    lane = lax.broadcasted_iota(jnp.int32, (tiles, tiles), 1)
    copies[0].wait()
    owner_row = owner[...].astype(F32)
    owner_col = jnp.transpose(jnp.broadcast_to(owner_row, (8, tiles)))[:, :1]
    earlier = (owner_col == owner_row) & (sub < lane)
    rank = jnp.sum(earlier.astype(F32), axis=0, keepdims=True)
    back = rank * 2 + owner_row * (2 * BACK_ROW)
    place_ref[...] = jnp.broadcast_to(back, (8, tiles)).astype(jnp.int32)
    dests = LANES // chunks
    rows = SLOT_DEV * dests
    sub = lax.broadcasted_iota(jnp.int32, (dests, tiles), 0).astype(F32)
    for k in range(chunks):
        mine = sub == owner_row - float(k * dests)
        for s in range(SLOT_DEV):
            at = k * rows + s * dests
            chosen[at : at + dests, :] = (mine & (rank == float(s))).astype(BF16)
    copies[1].wait()
    squares = jnp.sum(fold(jnp.square(grads[...])), axis=0, keepdims=True)
    box[pl.ds(message - 1, LANES, stride=message), :] = jnp.broadcast_to(squares, (LANES, LANES))
    terms = jnp.concatenate(two_terms(grads[...]), axis=0)
    for k in range(chunks):
        taken = chosen[k * rows : (k + 1) * rows, :]
        sent = dot(jnp.concatenate([taken, taken], axis=1), terms)
        for s in range(SLOT_DEV):
            for q in range(4):
                at = k * dests * message + q // 2 * OUT_ROW + 2 * s + q % 2
                box[pl.ds(at, dests, stride=message), :] = sent[
                    s * dests : (s + 1) * dests, q * LANES : (q + 1) * LANES
                ]


def clip_of(limit, box):
    squares = box[pl.ds(OUT_MESSAGE - 1, LANES, stride=OUT_MESSAGE), :]
    return limit / jnp.sqrt(total_of(squares))


def tile_of(box, s, clip, rows):
    for c in range(2):
        for parity in range(2):
            at = parity * OUT_ROW + 2 * s + c
            rows[c, pl.ds(parity, LANES, stride=2), :] = box[pl.ds(at, LANES, stride=OUT_MESSAGE), :] * clip
    return jnp.concatenate([rows[0], rows[1]], axis=1)


def shape_kernel(limit, chunks, box, left, right, moment, sent_hbm, ordered, sent, sems):
    clip = clip_of(limit, box)
    rows_of = sent.reshape(B, BACK_ROW, LANES)
    sums, out = [], []

    def send(half, pieces):
        ratios = []
        for adam_sum, shaped_sum in sums[4 * half : 4 * half + 4]:
            adam_mean = total_of(adam_sum) * (1.0 / (B * B))
            shaped_mean = total_of(shaped_sum) * (1.0 / (B * B))
            ratio = jnp.sqrt(adam_mean) / jnp.sqrt(shaped_mean + 1e-06)
            ratios.append(jnp.broadcast_to(ratio, (2, LANES)))
        ratios = jnp.concatenate(ratios, axis=0)
        rows = B // pieces
        for k in range(pieces):
            part = (pl.ds(k * rows, rows), pl.ds(8 * half, 8))
            rows_of[part] = rows_of[part] * ratios
            out.append(started(rows_of.at[part], sent_hbm.at[part], sems.at[len(out)]))

    for s in range(SLOT_DEV):
        tile = tile_of(box, s, clip, ordered.at[s])
        half = dot(left[s], tile.astype(BF16)).astype(BF16)
        shaped = dot(half, right[s])
        for c in range(2):
            sent[pl.ds(2 * s + c, B, stride=BACK_ROW), :] = shaped[:, c * LANES : (c + 1) * LANES]
        square = tile * tile
        moment_new = 0.9 * moment[s] + 0.1 * square
        sums.append((fold(square / moment_new), fold(shaped * shaped)))
        if s == 4:
            send(0, chunks[0])
    send(1, chunks[1])
    for copy in out:
        copy.wait()


def stats_kernel(limit, box, left, right, moment, left_out, right_out, moment_out, ordered):
    clip = clip_of(limit, box)
    s = pl.program_id(0)
    tile = tile_of(box, s, clip, ordered)
    moment_out[0] = 0.9 * moment[0] + 0.1 * (tile * tile)
    high = tile.astype(BF16)
    low = (tile - high.astype(F32)).astype(BF16)
    high_t, low_t = jnp.transpose(high), jnp.transpose(low)
    left_out[0] = 0.95 * left[0] + (dot(high, high_t) + (dot(high, low_t) + dot(low, high_t)))
    right_out[0] = 0.95 * right[0] + (dot(high_t, high) + (dot(high_t, low) + dot(low_t, high)))


def unpack_kernel(sizes, unroll, place, box, update_hbm, update, sems):
    first, out = 0, []
    for k, size in enumerate(sizes):

        def group(step, carry, first=first):
            for g in range(unroll):
                at_group = first + step * unroll + g
                rows = [place[at_group * 8 + j] for j in range(8)]
                for q in range(4):
                    at = q // 2 * BACK_ROW + q % 2
                    update[at_group, :, q * LANES : (q + 1) * LANES] = jnp.concatenate(
                        [box[pl.ds(row + at, 1), :] for row in rows], axis=0
                    )
            return carry

        lax.fori_loop(0, size // unroll, group, 0)
        part = pl.ds(first, size)
        out.append(started(update.at[part], update_hbm.at[part], sems.at[k]))
        first += size
    for copy in out:
        copy.wait()


def exchange(box):
    rows = box.reshape(box.shape[0], 1, LANES)
    rows = lax.all_to_all(rows, "shard", split_axis=0, concat_axis=0, tiled=True)
    return rows.reshape(box.shape)


def shards(grads, owner, left_stat, right_stat, left_root, right_root, moment):
    devices = lax.axis_size("shard")
    tiles, shard_len = grads.shape
    limit = math.sqrt(tiles * shard_len * devices)
    out_shape = (devices * OUT_MESSAGE, LANES)
    back_shape = (devices * 2 * BACK_ROW, LANES)
    update_shape = (tiles // 8, 8, shard_len)
    in_hbm = functools.partial(pltpu.with_memory_space_constraint, memory_space=pltpu.HBM)
    in_vmem = functools.partial(pltpu.with_memory_space_constraint, memory_space=pltpu.VMEM)
    slots = left_stat.shape
    dma = pltpu.SemaphoreType.DMA

    outbox, place = call(
        functools.partial(pack_kernel, 2), [HBM, HBM], [VMEM, VMEM],
        [pltpu.VMEM(out_shape, F32), jax.ShapeDtypeStruct((8, tiles), jnp.int32)],
        [pltpu.VMEM((1, tiles), jnp.int32), pltpu.VMEM(grads.shape, F32),
         pltpu.VMEM((devices * SLOT_DEV, tiles), BF16), dma((2,))],
        4 * tiles * devices * SLOT_DEV * shard_len, 16 * grads.size, 16,
    )(in_hbm(owner.reshape(1, tiles)), in_hbm(grads))
    place = place[0]
    arrived = exchange(outbox)

    sent = call(
        functools.partial(shape_kernel, limit, (2, 8)), [VMEM] * 4, HBM, pltpu.HBM((B, BACK_ROW, LANES), F32),
        [pltpu.VMEM((SLOT_DEV, 2, B, LANES), F32), pltpu.VMEM(back_shape, F32), dma((10,))],
        SLOT_DEV * 4 * B**3, SLOT_DEV * B * B * 16, 16,
    )(arrived, left_root, right_root, moment)
    returned = lax.all_to_all(sent.reshape(back_shape), "shard", split_axis=0, concat_axis=0, tiled=True)

    slot = pl.BlockSpec((1, B, B), lambda s: (s, 0, 0))
    left_new, right_new, moment_new = pl.pallas_call(
        functools.partial(stats_kernel, limit),
        grid=(SLOT_DEV,),
        in_specs=[VMEM] + [slot] * 3,
        out_specs=[slot] * 3,
        out_shape=[pltpu.HBM(slots, F32)] * 3,
        scratch_shapes=[pltpu.VMEM((2, B, LANES), F32)],
        cost_estimate=pl.CostEstimate(flops=SLOT_DEV * 12 * B**3, bytes_accessed=SLOT_DEV * B * B * 28, transcendentals=0),
        compiler_params=pltpu.CompilerParams(vmem_limit_bytes=8 * 1024 * 1024),
    )(in_hbm(arrived), in_hbm(left_stat), in_hbm(right_stat), in_hbm(moment))

    update = call(
        functools.partial(unpack_kernel, (24, 16, 8), 4), [SMEM, VMEM], HBM, jax.ShapeDtypeStruct(update_shape, F32),
        [pltpu.VMEM(update_shape, F32), dma((3,))], 2 * grads.size, 16 * grads.size, 8,
    )(place, in_vmem(returned))
    return (update.reshape(grads.shape), left_new, right_new, moment_new)


def solution(mesh):
    return jax.shard_map(
        shards,
        mesh=mesh,
        in_specs=(
            P(None, "shard"),
            P(),
            P("shard", None, None),
            P("shard", None, None),
            P("shard", None, None),
            P("shard", None, None),
            P("shard", None, None),
        ),
        out_specs=(
            P(None, "shard"),
            P("shard", None, None),
            P("shard", None, None),
            P("shard", None, None),
        ),
        check_vma=False,
    )
```

```python
import functools
import math

import jax
import jax.numpy as jnp
from jax import lax
from jax.experimental import pallas as pl
from jax.experimental.pallas import tpu as pltpu
from jax.sharding import PartitionSpec as P

B = 256
SLOT_DEV = 8
LANES = 128
OUT_ROW = 2 * SLOT_DEV
OUT_MESSAGE = 2 * OUT_ROW + 1
BACK_ROW = 2 * SLOT_DEV
ROOM_ROW = 3 * SLOT_DEV

HBM = pl.BlockSpec(memory_space=pltpu.HBM)
VMEM = pl.BlockSpec(memory_space=pltpu.VMEM)
SMEM = pl.BlockSpec(memory_space=pltpu.SMEM)
F32 = jnp.float32
BF16 = jnp.bfloat16


def call(kernel, in_specs, out_specs, out_shape, scratch, flops, bytes_accessed, vmem_mib=56):
    return pl.pallas_call(
        kernel,
        in_specs=in_specs,
        out_specs=out_specs,
        out_shape=out_shape,
        scratch_shapes=scratch,
        cost_estimate=pl.CostEstimate(flops=flops, bytes_accessed=bytes_accessed, transcendentals=0),
        compiler_params=pltpu.CompilerParams(vmem_limit_bytes=vmem_mib * 1024 * 1024),
    )


def started(source, target, sem):
    copy = pltpu.make_async_copy(source, target, sem)
    copy.start()
    return copy


def two_terms(x):
    high = x.astype(BF16)
    return high, (x - high.astype(F32)).astype(BF16)


def dot(a, b):
    return jnp.dot(a, b, preferred_element_type=F32)


def fold(x):
    total = jnp.sum(x.reshape(-1, 8, x.shape[1]), axis=0)
    return sum(total[:, lane : lane + LANES] for lane in range(0, x.shape[1], LANES))


def total_of(x):
    return jnp.sum(jnp.sum(x, axis=0, keepdims=True), axis=1, keepdims=True)


def pack_kernel(chunks, owner_hbm, grads_hbm, box, place_ref, owner, grads, chosen, sems):
    copies = [started(owner_hbm, owner, sems.at[0]), started(grads_hbm, grads, sems.at[1])]
    tiles = grads.shape[0]
    message = OUT_MESSAGE
    sub = lax.broadcasted_iota(jnp.int32, (tiles, tiles), 0)
    lane = lax.broadcasted_iota(jnp.int32, (tiles, tiles), 1)
    copies[0].wait()
    owner_row = owner[...].astype(F32)
    owner_col = jnp.transpose(jnp.broadcast_to(owner_row, (8, tiles)))[:, :1]
    earlier = (owner_col == owner_row) & (sub < lane)
    rank = jnp.sum(earlier.astype(F32), axis=0, keepdims=True)
    back = rank * 2 + owner_row * (2 * BACK_ROW)
    place_ref[...] = jnp.broadcast_to(back, (8, tiles)).astype(jnp.int32)
    dests = LANES // chunks
    rows = SLOT_DEV * dests
    sub = lax.broadcasted_iota(jnp.int32, (dests, tiles), 0).astype(F32)
    for k in range(chunks):
        mine = sub == owner_row - float(k * dests)
        for s in range(SLOT_DEV):
            at = k * rows + s * dests
            chosen[at : at + dests, :] = (mine & (rank == float(s))).astype(BF16)
    copies[1].wait()
    squares = jnp.sum(fold(jnp.square(grads[...])), axis=0, keepdims=True)
    box[pl.ds(message - 1, LANES, stride=message), :] = jnp.broadcast_to(squares, (LANES, LANES))
    terms = jnp.concatenate(two_terms(grads[...]), axis=0)
    for k in range(chunks):
        taken = chosen[k * rows : (k + 1) * rows, :]
        sent = dot(jnp.concatenate([taken, taken], axis=1), terms)
        for s in range(SLOT_DEV):
            for q in range(4):
                at = k * dests * message + q // 2 * OUT_ROW + 2 * s + q % 2
                box[pl.ds(at, dests, stride=message), :] = sent[
                    s * dests : (s + 1) * dests, q * LANES : (q + 1) * LANES
                ]


def clip_of(limit, box):
    squares = box[pl.ds(OUT_MESSAGE - 1, LANES, stride=OUT_MESSAGE), :]
    return limit / jnp.sqrt(total_of(squares))


def tile_of(box, s, clip, rows):
    for c in range(2):
        for parity in range(2):
            at = parity * OUT_ROW + 2 * s + c
            rows[c, pl.ds(parity, LANES, stride=2), :] = box[pl.ds(at, LANES, stride=OUT_MESSAGE), :] * clip
    return jnp.concatenate([rows[0], rows[1]], axis=1)


def shape_kernel(limit, chunks, box, left, right, moment, sent_hbm, ordered, sent, sems):
    clip = clip_of(limit, box)
    rows_of = sent.reshape(B, ROOM_ROW, LANES)
    sums, out = [], []

    def send(half, pieces):
        ratios = []
        for adam_sum, shaped_sum in sums[4 * half : 4 * half + 4]:
            adam_mean = total_of(adam_sum) * (1.0 / (B * B))
            shaped_mean = total_of(shaped_sum) * (1.0 / (B * B))
            ratio = jnp.sqrt(adam_mean) / jnp.sqrt(shaped_mean + 1e-06)
            ratios.append(jnp.broadcast_to(ratio, (2, LANES)))
        ratios = jnp.concatenate(ratios, axis=0)
        rows = B // pieces
        for k in range(pieces):
            part = (pl.ds(k * rows, rows), pl.ds(8 * half, 8))
            rows_of[part] = rows_of[part] * ratios
            out.append(started(rows_of.at[part], sent_hbm.at[part], sems.at[len(out)]))

    for s in range(SLOT_DEV):
        tile = tile_of(box, s, clip, ordered.at[s % 2])
        square = tile * tile
        moment_new = 0.9 * moment[s] + 0.1 * square
        adam_sum = fold(square / moment_new)
        half = dot(left[s], tile.astype(BF16)).astype(BF16)
        shaped = dot(half, right[s])
        for c in range(2):
            sent[pl.ds(2 * s + c, B, stride=ROOM_ROW), :] = shaped[:, c * LANES : (c + 1) * LANES]
        sums.append((adam_sum, fold(shaped * shaped)))
        if s == 4:
            send(0, chunks[0])
    send(1, chunks[1])
    for copy in out:
        copy.wait()


def stats_kernel(limit, box, left, right, moment, left_out, right_out, moment_out, ordered):
    clip = clip_of(limit, box)
    s = pl.program_id(0)
    tile = tile_of(box, s, clip, ordered)
    moment_out[0] = 0.9 * moment[0] + 0.1 * (tile * tile)
    high = tile.astype(BF16)
    low = (tile - high.astype(F32)).astype(BF16)
    high_t, low_t = jnp.transpose(high), jnp.transpose(low)
    left_out[0] = 0.95 * left[0] + (dot(high, high_t) + (dot(high, low_t) + dot(low, high_t)))
    right_out[0] = 0.95 * right[0] + (dot(high_t, high) + (dot(high_t, low) + dot(low_t, high)))


def unpack_kernel(sizes, unroll, place, box, update_hbm, update, sems):
    first, out = 0, []
    for k, size in enumerate(sizes):

        def group(step, carry, first=first):
            for g in range(unroll):
                at_group = first + step * unroll + g
                rows = [place[at_group * 8 + j] for j in range(8)]
                for q in range(4):
                    at = q // 2 * BACK_ROW + q % 2
                    update[at_group, :, q * LANES : (q + 1) * LANES] = jnp.concatenate(
                        [box[pl.ds(row + at, 1), :] for row in rows], axis=0
                    )
            return carry

        lax.fori_loop(0, size // unroll, group, 0)
        part = pl.ds(first, size)
        out.append(started(update.at[part], update_hbm.at[part], sems.at[k]))
        first += size
    for copy in out:
        copy.wait()


def exchange(box):
    rows = box.reshape(box.shape[0], 1, LANES)
    rows = lax.all_to_all(rows, "shard", split_axis=0, concat_axis=0, tiled=True)
    return rows.reshape(box.shape)


def shards(grads, owner, left_stat, right_stat, left_root, right_root, moment):
    devices = lax.axis_size("shard")
    tiles, shard_len = grads.shape
    limit = math.sqrt(tiles * shard_len * devices)
    out_shape = (devices * OUT_MESSAGE, LANES)
    back_shape = (devices * 2 * BACK_ROW, LANES)
    update_shape = (tiles // 8, 8, shard_len)
    in_hbm = functools.partial(pltpu.with_memory_space_constraint, memory_space=pltpu.HBM)
    in_vmem = functools.partial(pltpu.with_memory_space_constraint, memory_space=pltpu.VMEM)
    slots = left_stat.shape
    dma = pltpu.SemaphoreType.DMA

    outbox, place = call(
        functools.partial(pack_kernel, 2), [HBM, HBM], [VMEM, VMEM],
        [pltpu.VMEM(out_shape, F32), jax.ShapeDtypeStruct((8, tiles), jnp.int32)],
        [pltpu.VMEM((1, tiles), jnp.int32), pltpu.VMEM(grads.shape, F32),
         pltpu.VMEM((devices * SLOT_DEV, tiles), BF16), dma((2,))],
        4 * tiles * devices * SLOT_DEV * shard_len, 16 * grads.size, 16,
    )(in_hbm(owner.reshape(1, tiles)), in_hbm(grads))
    place = place[0]
    arrived = exchange(outbox)

    sent = call(
        functools.partial(shape_kernel, limit, (2, 4)), [VMEM] * 4, HBM, pltpu.HBM((B, BACK_ROW, LANES), F32),
        [pltpu.VMEM((2, 2, B, LANES), F32), pltpu.VMEM((B * ROOM_ROW, LANES), F32), dma((6,))],
        SLOT_DEV * 4 * B**3, SLOT_DEV * B * B * 16, 16,
    )(arrived, left_root, right_root, moment)
    returned = lax.all_to_all(sent.reshape(back_shape), "shard", split_axis=0, concat_axis=0, tiled=True)

    slot = pl.BlockSpec((1, B, B), lambda s: (s, 0, 0))
    left_new, right_new, moment_new = pl.pallas_call(
        functools.partial(stats_kernel, limit),
        grid=(SLOT_DEV,),
        in_specs=[VMEM] + [slot] * 3,
        out_specs=[slot] * 3,
        out_shape=[pltpu.HBM(slots, F32)] * 3,
        scratch_shapes=[pltpu.VMEM((2, B, LANES), F32)],
        cost_estimate=pl.CostEstimate(flops=SLOT_DEV * 12 * B**3, bytes_accessed=SLOT_DEV * B * B * 28, transcendentals=0),
        compiler_params=pltpu.CompilerParams(vmem_limit_bytes=8 * 1024 * 1024),
    )(in_hbm(arrived), in_hbm(left_stat), in_hbm(right_stat), in_hbm(moment))

    update = call(
        functools.partial(unpack_kernel, (24, 16, 8), 4), [SMEM, VMEM], HBM, jax.ShapeDtypeStruct(update_shape, F32),
        [pltpu.VMEM(update_shape, F32), dma((3,))], 2 * grads.size, 16 * grads.size, 8,
    )(place, in_vmem(returned))
    return (update.reshape(grads.shape), left_new, right_new, moment_new)


def solution(mesh):
    return jax.shard_map(
        shards,
        mesh=mesh,
        in_specs=(
            P(None, "shard"),
            P(),
            P("shard", None, None),
            P("shard", None, None),
            P("shard", None, None),
            P("shard", None, None),
            P("shard", None, None),
        ),
        out_specs=(
            P(None, "shard"),
            P("shard", None, None),
            P("shard", None, None),
            P("shard", None, None),
        ),
        check_vma=False,
    )
```

```python
import functools
import math

import jax
import jax.numpy as jnp
from jax import lax
from jax.experimental import pallas as pl
from jax.experimental.pallas import tpu as pltpu
from jax.sharding import PartitionSpec as P

B = 256
SLOT_DEV = 8
LANES = 128
OUT_ROW = 2 * SLOT_DEV
OUT_MESSAGE = 2 * OUT_ROW + 1
BACK_ROW = 2 * SLOT_DEV
ROOM_ROW = 3 * SLOT_DEV

HBM = pl.BlockSpec(memory_space=pltpu.HBM)
VMEM = pl.BlockSpec(memory_space=pltpu.VMEM)
SMEM = pl.BlockSpec(memory_space=pltpu.SMEM)
F32 = jnp.float32
BF16 = jnp.bfloat16


def call(kernel, in_specs, out_specs, out_shape, scratch, flops, bytes_accessed, vmem_mib=56):
    return pl.pallas_call(
        kernel,
        in_specs=in_specs,
        out_specs=out_specs,
        out_shape=out_shape,
        scratch_shapes=scratch,
        cost_estimate=pl.CostEstimate(flops=flops, bytes_accessed=bytes_accessed, transcendentals=0),
        compiler_params=pltpu.CompilerParams(vmem_limit_bytes=vmem_mib * 1024 * 1024),
    )


def started(source, target, sem):
    copy = pltpu.make_async_copy(source, target, sem)
    copy.start()
    return copy


def two_terms(x):
    high = x.astype(BF16)
    return high, (x - high.astype(F32)).astype(BF16)


def dot(a, b):
    return jnp.dot(a, b, preferred_element_type=F32)


def fold(x):
    total = jnp.sum(x.reshape(-1, 8, x.shape[1]), axis=0)
    return sum(total[:, lane : lane + LANES] for lane in range(0, x.shape[1], LANES))


def total_of(x):
    return jnp.sum(jnp.sum(x, axis=0, keepdims=True), axis=1, keepdims=True)


def pack_kernel(chunks, owner_hbm, grads_hbm, box, place_ref, owner, grads, chosen, sems):
    copies = [started(owner_hbm, owner, sems.at[0]), started(grads_hbm, grads, sems.at[1])]
    tiles = grads.shape[0]
    message = OUT_MESSAGE
    sub = lax.broadcasted_iota(jnp.int32, (tiles, tiles), 0)
    lane = lax.broadcasted_iota(jnp.int32, (tiles, tiles), 1)
    copies[0].wait()
    owner_row = owner[...].astype(F32)
    owner_col = jnp.transpose(jnp.broadcast_to(owner_row, (8, tiles)))[:, :1]
    earlier = (owner_col == owner_row) & (sub < lane)
    rank = jnp.sum(earlier.astype(F32), axis=0, keepdims=True)
    back = rank * 2 + owner_row * (2 * BACK_ROW)
    place_ref[...] = jnp.broadcast_to(back, (8, tiles)).astype(jnp.int32)
    dests = LANES // chunks
    rows = SLOT_DEV * dests
    sub = lax.broadcasted_iota(jnp.int32, (dests, tiles), 0).astype(F32)
    for k in range(chunks):
        mine = sub == owner_row - float(k * dests)
        for s in range(SLOT_DEV):
            at = k * rows + s * dests
            chosen[at : at + dests, :] = (mine & (rank == float(s))).astype(BF16)
    copies[1].wait()
    squares = jnp.sum(fold(jnp.square(grads[...])), axis=0, keepdims=True)
    box[pl.ds(message - 1, LANES, stride=message), :] = jnp.broadcast_to(squares, (LANES, LANES))
    terms = jnp.concatenate(two_terms(grads[...]), axis=0)
    for k in range(chunks):
        taken = chosen[k * rows : (k + 1) * rows, :]
        sent = dot(jnp.concatenate([taken, taken], axis=1), terms)
        for s in range(SLOT_DEV):
            for q in range(4):
                at = k * dests * message + q // 2 * OUT_ROW + 2 * s + q % 2
                box[pl.ds(at, dests, stride=message), :] = sent[
                    s * dests : (s + 1) * dests, q * LANES : (q + 1) * LANES
                ]


def clip_of(limit, box):
    squares = box[pl.ds(OUT_MESSAGE - 1, LANES, stride=OUT_MESSAGE), :]
    return limit / jnp.sqrt(total_of(squares))


def tile_of(box, s, clip, rows):
    for c in range(2):
        for parity in range(2):
            at = parity * OUT_ROW + 2 * s + c
            rows[c, pl.ds(parity, LANES, stride=2), :] = box[pl.ds(at, LANES, stride=OUT_MESSAGE), :] * clip
    return jnp.concatenate([rows[0], rows[1]], axis=1)


def shape_kernel(limit, chunks, box, left, right, moment, sent_hbm, ordered, sent, sems):
    clip = clip_of(limit, box)
    rows_of = sent.reshape(B, ROOM_ROW, LANES)
    sums, out = [], []

    def send(half, pieces):
        ratios = []
        for adam_sum, shaped_sum in sums[4 * half : 4 * half + 4]:
            adam_mean = total_of(adam_sum) * (1.0 / (B * B))
            shaped_mean = total_of(shaped_sum) * (1.0 / (B * B))
            ratio = jnp.sqrt(adam_mean) / jnp.sqrt(shaped_mean + 1e-06)
            ratios.append(jnp.broadcast_to(ratio, (2, LANES)))
        ratios = jnp.concatenate(ratios, axis=0)
        rows = B // pieces
        for k in range(pieces):
            part = (pl.ds(k * rows, rows), pl.ds(8 * half, 8))
            rows_of[part] = rows_of[part] * ratios
            out.append(started(rows_of.at[part], sent_hbm.at[part], sems.at[len(out)]))

    for s in range(SLOT_DEV):
        tile = tile_of(box, s, clip, ordered.at[s % 2])
        square = tile * tile
        moment_new = 0.9 * moment[s] + 0.1 * square
        adam_sum = fold(square / moment_new)
        half = dot(left[s], tile.astype(BF16)).astype(BF16)
        shaped = dot(half, right[s])
        for c in range(2):
            sent[pl.ds(2 * s + c, B, stride=ROOM_ROW), :] = shaped[:, c * LANES : (c + 1) * LANES]
        sums.append((adam_sum, fold(shaped * shaped)))
        if s == 4:
            send(0, chunks[0])
    send(1, chunks[1])
    for copy in out:
        copy.wait()


def stats_kernel(limit, box, left, right, moment, left_out, right_out, moment_out, ordered):
    clip = clip_of(limit, box)
    s = pl.program_id(0)
    tile = tile_of(box, s, clip, ordered)
    moment_out[0] = 0.9 * moment[0] + 0.1 * (tile * tile)
    high = tile.astype(BF16)
    low = (tile - high.astype(F32)).astype(BF16)
    high_t, low_t = jnp.transpose(high), jnp.transpose(low)
    left_out[0] = 0.95 * left[0] + (dot(high, high_t) + (dot(high, low_t) + dot(low, high_t)))
    right_out[0] = 0.95 * right[0] + (dot(high_t, high) + (dot(high_t, low) + dot(low_t, high)))


def unpack_kernel(sizes, unroll, place, box, update_hbm, update, sems):
    first, out = 0, []
    for k, size in enumerate(sizes):

        def group(step, carry, first=first):
            for g in range(unroll):
                at_group = first + step * unroll + g
                rows = [place[at_group * 8 + j] for j in range(8)]
                for parity in range(2):
                    halves = [box[pl.ds(row + parity * BACK_ROW, 2), :] for row in rows]
                    for c in range(2):
                        lane = (2 * parity + c) * LANES
                        update[at_group, :, lane : lane + LANES] = jnp.concatenate(
                            [half[c : c + 1] for half in halves], axis=0
                        )
            return carry

        lax.fori_loop(0, size // unroll, group, 0)
        part = pl.ds(first, size)
        out.append(started(update.at[part], update_hbm.at[part], sems.at[k]))
        first += size
    for copy in out:
        copy.wait()


def exchange(box):
    rows = box.reshape(box.shape[0], 1, LANES)
    rows = lax.all_to_all(rows, "shard", split_axis=0, concat_axis=0, tiled=True)
    return rows.reshape(box.shape)


def shards(grads, owner, left_stat, right_stat, left_root, right_root, moment):
    devices = lax.axis_size("shard")
    tiles, shard_len = grads.shape
    limit = math.sqrt(tiles * shard_len * devices)
    out_shape = (devices * OUT_MESSAGE, LANES)
    back_shape = (devices * 2 * BACK_ROW, LANES)
    update_shape = (tiles // 8, 8, shard_len)
    in_hbm = functools.partial(pltpu.with_memory_space_constraint, memory_space=pltpu.HBM)
    in_vmem = functools.partial(pltpu.with_memory_space_constraint, memory_space=pltpu.VMEM)
    slots = left_stat.shape
    dma = pltpu.SemaphoreType.DMA

    outbox, place = call(
        functools.partial(pack_kernel, 2), [HBM, HBM], [VMEM, VMEM],
        [pltpu.VMEM(out_shape, F32), jax.ShapeDtypeStruct((8, tiles), jnp.int32)],
        [pltpu.VMEM((1, tiles), jnp.int32), pltpu.VMEM(grads.shape, F32),
         pltpu.VMEM((devices * SLOT_DEV, tiles), BF16), dma((2,))],
        4 * tiles * devices * SLOT_DEV * shard_len, 16 * grads.size, 16,
    )(in_hbm(owner.reshape(1, tiles)), in_hbm(grads))
    place = place[0]
    arrived = exchange(outbox)

    sent = call(
        functools.partial(shape_kernel, limit, (2, 4)), [VMEM] * 4, HBM, pltpu.HBM((B, BACK_ROW, LANES), F32),
        [pltpu.VMEM((2, 2, B, LANES), F32), pltpu.VMEM((B * ROOM_ROW, LANES), F32), dma((6,))],
        SLOT_DEV * 4 * B**3, SLOT_DEV * B * B * 16, 16,
    )(arrived, left_root, right_root, moment)
    returned = lax.all_to_all(sent.reshape(back_shape), "shard", split_axis=0, concat_axis=0, tiled=True)

    slot = pl.BlockSpec((1, B, B), lambda s: (s, 0, 0))
    left_new, right_new, moment_new = pl.pallas_call(
        functools.partial(stats_kernel, limit),
        grid=(SLOT_DEV,),
        in_specs=[VMEM] + [slot] * 3,
        out_specs=[slot] * 3,
        out_shape=[pltpu.HBM(slots, F32)] * 3,
        scratch_shapes=[pltpu.VMEM((2, B, LANES), F32)],
        cost_estimate=pl.CostEstimate(flops=SLOT_DEV * 12 * B**3, bytes_accessed=SLOT_DEV * B * B * 28, transcendentals=0),
        compiler_params=pltpu.CompilerParams(vmem_limit_bytes=8 * 1024 * 1024),
    )(in_hbm(arrived), in_hbm(left_stat), in_hbm(right_stat), in_hbm(moment))

    update = call(
        functools.partial(unpack_kernel, (24, 16, 8), 8), [SMEM, VMEM], HBM, jax.ShapeDtypeStruct(update_shape, F32),
        [pltpu.VMEM(update_shape, F32), dma((3,))], 2 * grads.size, 16 * grads.size, 8,
    )(place, in_vmem(returned))
    return (update.reshape(grads.shape), left_new, right_new, moment_new)


def solution(mesh):
    return jax.shard_map(
        shards,
        mesh=mesh,
        in_specs=(
            P(None, "shard"),
            P(),
            P("shard", None, None),
            P("shard", None, None),
            P("shard", None, None),
            P("shard", None, None),
            P("shard", None, None),
        ),
        out_specs=(
            P(None, "shard"),
            P("shard", None, None),
            P("shard", None, None),
            P("shard", None, None),
        ),
        check_vma=False,
    )
```
